256 devices in a mesh: layer: 8 (over y, core), expert: 32 (over z, x).
Axes of the slice: x: 4, y: 4, z: 8, core: 2. Of those that a mesh axis runs over, the one named last changes fastest.
Arguments:
- stream_in: bfloat16 [4, 1024, 3584], P(None, 'expert'), may hold values from -6 to 6
- gain: float32 [8, 3584], P('layer'), may hold values from 0.5 to 1.5
- w_gate: bfloat16 [8, 3584, 8192], P('layer', None, 'expert'), may hold values from -0.09375 to 0.09375
- w_up: bfloat16 [8, 3584, 8192], P('layer', None, 'expert'), may hold values from -0.09375 to 0.09375
- w_down: bfloat16 [8, 8192, 3584], P('layer', 'expert'), may hold values from -0.125 to 0.125
- routes: int32 [8, 4, 1024, 8], P('layer', None, 'expert'), may hold values from 0 to 255, all different within a row; in each aligned block of 32 rows (0 to 31, 32 to 63, ..., all dimensions but the last counted through in order) at most 2 rows name the same one
- gates: float32 [8, 4, 1024, 8], P('layer', None, 'expert'), may hold values from 0.2 to 1
Outputs:
- layer_out: bfloat16 [8, 4, 1024, 3584], P('layer', None, 'expert')
- hessian: float32 [8, 8192, 2048], P('layer', 'expert')
The draws below stay inside these ranges and needn't reach their ends.
Inputs may be any that keep to these rules, and one draw needn't show every extreme that they name: `routes`: each token names 8 different experts; in each aligned block of 32 tokens (the rows of one device) no expert is named by more than 2 tokens.
All inputs are finite; a program needn't handle non-finite values.
Results may differ from the reference program's by a relative error of at most 0.014.
Values may be sent and summed in bfloat16 or wider, within the bound.
A program may use at most 64 MiB of HBM per device.

```python
import math
import jax
import jax.numpy as jnp
import numpy as np
from jax import lax

D = 3584
FF = 2048
EXPERTS = 256
TOP = 8
GROUP = 8
FRONTS = 4
TOK_DEV = 32
CAP = 2
LAYERS = 8
FLIGHT = 4
TOKENS = 1024
N_EXPERT = 32


def block_scale(rng, shape, cuts, low, top_value):
    level = 1.0
    for axis_at, blocks in cuts:
        steps = jax.random.uniform(jax.random.fold_in(jax.random.fold_in(rng, 6), axis_at), (blocks,), jnp.float32, low / len(cuts), top_value / len(cuts))
        level = level * jnp.repeat(jnp.exp(steps), shape[axis_at] // blocks).reshape((-1,) + (1,) * (len(shape) - 1 - axis_at))
    return level


def routed_block(own_key, own, number, rows, count, top, reach, skew):
    sequence = jax.random.permutation(own_key, count)
    packed, ordinary = shares(count, rows * top, reach, skew, True), shares(count, rows * top, reach, skew, False)
    places = jnp.arange(count)

    def named(sizes, turn):
        used = int((sizes > 0).sum())
        fixed = max(1, used // 4)
        passed = fixed + (places - fixed + turn * (used - fixed)) % max(1, count - fixed)
        return jnp.zeros((count,), jnp.int32).at[sequence[jnp.where(places < fixed, places, passed)]].set(jnp.asarray(sizes, jnp.int32))

    sizes = jnp.where(number % 4 == 0, named(packed, number // 4), named(ordinary, number - number // 4 - 1))
    mixed = jax.random.permutation(jax.random.fold_in(own, 3), count)
    source_of, taker = mixed[0:count // 2 * 2:2], mixed[1:count // 2 * 2:2]
    room = jnp.minimum(sizes[source_of] - 1, reach - sizes[taker]) // 2
    room = jnp.where((source_of == sequence[0]) | (taker == sequence[0]) | (sizes[taker] == 0), 0, jnp.maximum(room, 0))
    passed = jax.random.randint(jax.random.fold_in(own, 4), (count // 2,), 0, 1 << 20) % (room + 1)
    sizes = sizes.at[source_of].add(-passed).at[taker].add(passed)
    items = jnp.searchsorted(jnp.cumsum(sizes), jnp.arange(rows * top), side="right").astype(jnp.int32)
    table = items.reshape(top, rows).T
    table = table[jax.random.permutation(jax.random.fold_in(own, 1), rows)]
    turn = jax.random.randint(jax.random.fold_in(own, 2), (rows, 1), 0, top)
    return jnp.take_along_axis(table, (jnp.arange(top)[None, :] + turn) % top, axis=1)


def shares(count, total, reach, slope, full):
    weights = [(1 << 20) // math.isqrt(standing ** slope) + 1 for standing in range(1, count + 1)]
    largest = reach if full else min(reach, max(-(-total // count), total * weights[0] // sum(weights)))
    least = 1 if total - largest >= count - 1 else 0
    counts, spare = [largest] + [least] * (count - 1), total - largest - least * (count - 1)
    while spare > 0:
        free = [i for i in range(1, count) if counts[i] < largest] or [i for i in range(1, count) if counts[i] < reach]
        whole, remaining = sum([weights[i] for i in free]), spare
        for i in free:
            addition = min(reach - counts[i], max(1, remaining * weights[i] // whole), spare)
            counts[i] = counts[i] + addition
            spare = spare - addition
    return np.array(counts)


def normal_values(key, dims, scale, limit, cuts=(), held_as=jnp.bfloat16):
    drawn = scale * jax.random.normal(key, dims, jnp.float32)
    if cuts:
        drawn = drawn * block_scale(key, dims, cuts, -0.22, 0.18)
    return jnp.clip(drawn, -limit, limit).astype(held_as)


def setup_inputs(seed: int = 0) -> dict:
    key_of = jax.random.split(jax.random.key(seed), 8)
    stream_in = normal_values(key_of[0], (FRONTS, TOKENS, D), 1.0, 6.0, ((1, 32),))
    gain = jnp.clip(1.0 + 0.1 * jax.random.normal(key_of[1], (LAYERS, D), jnp.float32), 0.5, 1.5)
    w_gate = normal_values(key_of[2], (LAYERS, D, FLIGHT * FF), D ** -0.5, 0.09375, ((0, 8), (2, 32)))
    w_up = normal_values(key_of[3], (LAYERS, D, FLIGHT * FF), D ** -0.5, 0.09375, ((0, 8), (2, 32)))
    w_down = normal_values(key_of[4], (LAYERS, FLIGHT * FF, D), FF ** -0.5, 0.125, ((0, 8), (1, 32)))
    routes_keys = jax.random.split(jax.random.fold_in(key_of[5], 1), LAYERS * FRONTS * TOKENS // TOK_DEV)
    routes_turns = jax.random.permutation(jax.random.fold_in(key_of[5], 3), LAYERS * FRONTS * TOKENS // TOK_DEV)
    routes = jax.vmap(lambda own, number: routed_block(jax.random.fold_in(key_of[5], 2), own, number, TOK_DEV, EXPERTS, TOP, CAP, 2))(routes_keys, routes_turns).reshape((LAYERS, FRONTS, TOKENS, TOP))
    gates = jnp.clip(0.2 + 0.8 * jax.random.uniform(key_of[6], (LAYERS, FRONTS, TOKENS, TOP), jnp.float32) ** block_scale(key_of[6], (LAYERS, FRONTS, TOKENS, TOP), ((0, 8), (2, 32)), -0.2, 0.2), 0.2, 1.0)
    return {"stream_in": stream_in, "gain": gain, "w_gate": w_gate, "w_up": w_up, "w_down": w_down, "routes": routes, "gates": gates}


EPSILON = 1e-06

def reference(stream_in, gain, w_gate, w_up, w_down, routes, gates):
    flight = N_EXPERT // GROUP
    units = FF // GROUP
    rows_all = N_EXPERT * CAP
    state = stream_in
    layer_outputs = []
    grams = []
    for layer in range(LAYERS):
        gram_parts = [jnp.zeros((FF, FF), jnp.float32) for expert in range(flight)]
        fronts_out = []
        for front in range(FRONTS):
            wide = state[front].astype(jnp.float32)
            scale = lax.rsqrt(lax.optimization_barrier(jnp.mean(wide * wide, axis=-1, keepdims=True)) + EPSILON)
            normed = (wide * scale * gain[layer]).astype(jnp.bfloat16)
            update = jnp.zeros((TOKENS, D), jnp.float32)
            for expert in range(flight):
                matches = routes[layer, front] == expert
                routed = jnp.any(matches, axis=1)
                weight = lax.optimization_barrier(jnp.sum(jnp.where(matches, gates[layer, front], 0.0), axis=1))
                blocks = routed.astype(jnp.int32).reshape(N_EXPERT, TOK_DEV)
                place = (jnp.cumsum(blocks, axis=1) - 1).reshape(TOKENS).astype(jnp.int32)
                owner = jnp.arange(TOKENS, dtype=jnp.int32) // TOK_DEV
                target = jnp.where(routed, owner * CAP + place, rows_all).astype(jnp.int32)
                gathered = jnp.zeros((rows_all + 1, D), jnp.bfloat16).at[target].set(normed)[:rows_all]
                low = expert * FF
                gate_act = jnp.dot(gathered, w_gate[layer][:, low:low + FF], preferred_element_type=jnp.float32)
                up_act = jnp.dot(gathered, w_up[layer][:, low:low + FF], preferred_element_type=jnp.float32)
                hidden = (jax.nn.silu(gate_act) * up_act).astype(jnp.bfloat16)
                gram_parts[expert] = gram_parts[expert] + jnp.dot(hidden.T, hidden, preferred_element_type=jnp.float32)
                total = jnp.zeros((rows_all, D), jnp.float32)
                for member in range(GROUP):
                    first = low + member * units
                    piece = jnp.dot(hidden[:, member * units:(member + 1) * units], w_down[layer][first:first + units], preferred_element_type=jnp.float32).astype(jnp.bfloat16)
                    total = total + lax.optimization_barrier(piece).astype(jnp.float32)
                padded = jnp.concatenate([total, jnp.zeros((1, D), jnp.float32)], axis=0)
                update = update + weight[:, None] * padded[target]
            fronts_out.append((wide + update).astype(jnp.bfloat16))
        state = jnp.stack(fronts_out)
        layer_outputs.append(state)
        grams.append(jnp.concatenate(gram_parts, axis=0) * (1.0 / (FRONTS * CAP)))
    return (jnp.stack(layer_outputs), jnp.stack(grams))
```

```python
import functools

import jax
import jax.numpy as jnp
from jax import lax
from jax.experimental import pallas as pl
from jax.experimental.pallas import tpu as pltpu
from jax.sharding import PartitionSpec as P

GROUP = 8
CAP = 2
EPSILON = 1e-06
MESH = pl.DeviceIdType.MESH
PLANES = 8
RING = 4
BF16 = jnp.bfloat16
F32 = jnp.float32


def first_and_second(route, expert, lanes):
    routed = jnp.max((route == expert).astype(F32), axis=0, keepdims=True)
    first = jnp.min(jnp.where(routed > 0, lanes, 1000), axis=1, keepdims=True)
    slot0 = jnp.where(lanes == first, routed, 0.0)
    return slot0, routed - slot0


def kernel(
    stream, gain, wg, wu, wd, routes, gates,
    out, hess,
    wg_v, wu_v, wd_v, routes_next,
    pick_own, mix_full, mix_next,
    xin, xout, sbuf, abuf, arecv, rows, part, drecv, ebuf, erecv, hid, gram,
    w_sem, in_sem, out_sem, hess_sem,
    r_send, r_recv, s_send, a_send, a_recv, b_send, b_recv,
    h_send, h_recv, d_send, d_recv, e_send, e_recv, x_send, x_recv,
):
    fronts, tokens, width = xin.shape
    flight = PLANES // 2
    sections = lax.axis_size("layer")
    layer = lax.axis_index("layer")
    place = lax.axis_index("expert")
    z, x = place // RING, place % RING
    half = z % 2
    member = half * RING + x
    is_first, is_last = layer == 0, layer == sections - 1

    def at_z(step):
        return lax.rem(z + step, PLANES)

    def at_x(step):
        return lax.rem(x + step, RING)

    def peers():
        group = []
        for other in (0, 1):
            for step in range(RING):
                if other or step:
                    p = lax.rem(half + other, 2)
                    nx = at_x(step)
                    group.append(((z - half + p) * RING + nx, p * RING + nx))
        return group

    group = peers()

    def remote(src, dst, send, recv, to_layer, to_place):
        return pltpu.make_async_remote_copy(
            src_ref=src, dst_ref=dst, send_sem=send, recv_sem=recv,
            device_id=(to_layer, to_place), device_id_type=MESH,
        )

    def copy_routes(to_layer):
        return remote(routes, routes_next, r_send, r_recv, to_layer, place)

    def copy_s(f, to_z):
        return remote(sbuf.at[f, to_z // 2], arecv.at[f, z], s_send.at[f, to_z], a_recv.at[f, z],
                      layer, to_z * RING + x)

    def copy_a(f, to_z, slot, to_layer):
        return remote(abuf.at[f, to_z // 2], arecv.at[f, slot], a_send.at[f, to_z], a_recv.at[f, slot],
                      to_layer, to_z * RING + x)

    def copy_b(f, to_x, slot):
        return remote(rows.at[f, slot], rows.at[f, slot], b_send.at[f, to_x], b_recv.at[f, slot],
                      layer, z * RING + to_x)

    def copy_h(f, to_place, to_member, slot):
        return remote(hid.at[slot, f], hid.at[slot, f], h_send.at[f, to_member], h_recv.at[f, slot],
                      layer, to_place)

    def copy_d(f, to_x, slot):
        return remote(part.at[f, to_x], drecv.at[f, slot], d_send.at[f, to_x], d_recv.at[f, slot],
                      layer, z * RING + to_x)

    def copy_e(f, to_z, slot):
        return remote(ebuf.at[f, to_z], erecv.at[f, slot], e_send.at[f, to_z], e_recv.at[f, slot],
                      layer, to_z * RING + x)

    def copy_x(f, to_layer):
        return remote(xout.at[f], xin.at[f], x_send.at[f], x_recv.at[f], to_layer, place)

    def load_stream(f):
        return pltpu.make_async_copy(stream.at[f], xin.at[f], in_sem.at[f])

    def store_out(f):
        return pltpu.make_async_copy(xout.at[f], out.at[0, f], out_sem.at[f])

    weights = (
        pltpu.make_async_copy(wg.at[0], wg_v, w_sem.at[0]),
        pltpu.make_async_copy(wu.at[0], wu_v, w_sem.at[1]),
        pltpu.make_async_copy(wd.at[0], wd_v, w_sem.at[2]),
    )

    @pl.when(is_first)
    def _():
        for f in range(fronts):
            load_stream(f).start()

    for load in weights:
        load.start()

    barrier = pltpu.get_barrier_semaphore()

    def greet(to_layer, to_place):
        pl.semaphore_signal(barrier, inc=1, device_id=(to_layer, to_place), device_id_type=MESH)

    @pl.when(layer > 0)
    def _():
        for step in range(PLANES):
            greet(layer - 1, at_z(step) * RING + x)

    @pl.when(layer < sections - 1)
    def _():
        greet(layer + 1, place)

    for step in range(1, PLANES):
        greet(layer, at_z(step) * RING + x)
    for step in range(1, RING):
        greet(layer, z * RING + at_x(step))
    for step in range(1, RING):
        greet(layer, (z - half + (1 - half)) * RING + at_x(step))

    lanes = lax.broadcasted_iota(jnp.int32, (1, tokens), 1)
    row8 = lax.broadcasted_iota(jnp.int32, (flight * CAP, tokens), 0)
    row16 = lax.broadcasted_iota(jnp.int32, (2 * flight * CAP, tokens), 0)
    eye = (
        lax.broadcasted_iota(jnp.int32, (tokens, tokens), 0)
        == lax.broadcasted_iota(jnp.int32, (tokens, tokens), 1)
    ).astype(BF16)

    def own_tables(f):
        route, gate = routes[f], gates[f]
        pick = jnp.zeros((flight * CAP, tokens), F32)
        scaled = jnp.zeros((2 * flight * CAP, tokens), F32)
        for expert in range(flight):
            slots = first_and_second(route, expert, lanes)
            weight = jnp.sum(jnp.where(route == expert, gate, 0.0), axis=0, keepdims=True)
            for c in range(CAP):
                pick = jnp.where(row8 == expert * CAP + c, slots[c], pick)
                here = jnp.logical_and(row16 // (2 * CAP) == expert, row16 % CAP == c)
                scaled = jnp.where(here, slots[c] * weight, scaled)
        pick_own[f] = pick.astype(BF16)
        mix = scaled.T
        high = mix.astype(BF16)
        low = (mix - high.astype(F32)).astype(BF16)
        mix_full[f] = jnp.concatenate([eye, high, low], axis=1)

    def next_tables(f):
        route = routes_next[f]
        pick = jnp.zeros((flight * CAP, tokens), F32)
        for expert in range(flight):
            slots = first_and_second(route, expert, lanes)
            for c in range(CAP):
                pick = jnp.where(row8 == expert * CAP + c, slots[c], pick)
        mix_next[f] = jnp.dot(
            pick.astype(BF16), mix_full[f], preferred_element_type=F32
        ).astype(BF16)

    for f in range(fronts):
        own_tables(f)

    @pl.when(jnp.logical_and(is_first, is_last))
    def _():
        pl.semaphore_wait(barrier, 13)

    @pl.when(jnp.logical_and(is_first, jnp.logical_not(is_last)))
    def _():
        pl.semaphore_wait(barrier, 13 + PLANES)

    @pl.when(jnp.logical_and(jnp.logical_not(is_first), is_last))
    def _():
        pl.semaphore_wait(barrier, 13 + 1)

    @pl.when(jnp.logical_and(jnp.logical_not(is_first), jnp.logical_not(is_last)))
    def _():
        pl.semaphore_wait(barrier, 13 + 1 + PLANES)

    @pl.when(layer > 0)
    def _():
        copy_routes(layer - 1).start()

    def stage_s(f):
        load_stream(f).wait()
        picked = jnp.dot(pick_own[f], xin[f], preferred_element_type=F32).astype(BF16)
        sbuf[f] = picked.reshape(flight, CAP, width)
        for step in range(1, PLANES):
            copy_s(f, at_z(step)).start()
        arecv[f, z] = sbuf[f, z // 2]

    def stage_a(f):
        for step in range(1, PLANES):
            copy_a(f, z, at_z(step), layer).wait_recv()

        @pl.when(layer > 0)
        def _():
            copy_a(f, z, z, layer).wait_recv()

        wide = arecv[f].reshape(PLANES * CAP, width).astype(F32)
        scale = lax.rsqrt(jnp.mean(wide * wide, axis=-1, keepdims=True) + EPSILON)
        rows[f, x] = (wide * scale * gain[...]).astype(BF16)
        for step in (2, 1, 3):
            copy_b(f, at_x(step), x).start()

    def stage_b(f):
        for step in range(1, RING):
            copy_b(f, x, at_x(step)).wait_recv()
        all_rows = rows[f].reshape(RING * PLANES * CAP, width)
        gate_act = jnp.dot(all_rows, wg_v[...], preferred_element_type=F32)
        up_act = jnp.dot(all_rows, wu_v[...], preferred_element_type=F32)
        hidden = (jax.nn.silu(gate_act) * up_act).astype(BF16)
        partial = jnp.dot(hidden, wd_v[...], preferred_element_type=F32).astype(BF16)
        part[f] = partial.reshape(RING, PLANES * CAP, width)
        for step in (2, 1, 3):
            copy_d(f, at_x(step), x).start()
        hid[member, f] = hidden
        for to_place, to_member in group:
            copy_h(f, to_place, to_member, member).start()

    def stage_d(f):
        for step in range(1, RING):
            copy_d(f, x, at_x(step)).wait_recv()
        total = part[f, x].astype(F32)
        for step in range(1, RING):
            total = total + drecv[f, at_x(step)].astype(F32)
        ebuf[f] = total.astype(BF16).reshape(PLANES, CAP, width)
        for step in range(1, PLANES):
            copy_e(f, at_z(step), z).start()
        erecv[f, z] = ebuf[f, z]

    def stage_e(f):
        @pl.when(layer > 0)
        def _():
            copy_x(f, layer).wait_recv()

        for step in range(1, PLANES):
            copy_e(f, z, at_z(step)).wait_recv()
        returned = erecv[f].reshape(PLANES * CAP, width)
        stack = jnp.concatenate([xin[f], returned, returned], axis=0)

        @pl.when(layer < sections - 1)
        def _():
            picked = jnp.dot(mix_next[f], stack, preferred_element_type=F32).astype(BF16)
            abuf[f] = picked.reshape(flight, CAP, width)
            for step in range(PLANES):
                copy_a(f, at_z(step), z, layer + 1).start()

        xout[f] = jnp.dot(mix_full[f], stack, preferred_element_type=F32).astype(BF16)

        @pl.when(layer < sections - 1)
        def _():
            copy_x(f, layer + 1).start()

        store_out(f).start()

    @pl.when(is_first)
    def _():
        stage_s(0)

    @pl.when(layer < sections - 1)
    def _():
        copy_routes(layer).wait_recv()
        for f in range(fronts):
            next_tables(f)

    for load in weights:
        load.wait()

    stage_a(0)

    @pl.when(is_first)
    def _():
        stage_s(1)

    stage_b(0)

    @pl.when(is_first)
    def _():
        for f in range(2, fronts):
            stage_s(f)

    def steady(f, carry):
        stage_d(f)
        stage_a(f + 1)
        stage_e(f)
        stage_b(f + 1)
        return carry

    lax.fori_loop(0, fronts - 1, steady, 0)
    stage_d(fronts - 1)

    for f in range(fronts):
        for _, slot in group:
            copy_h(f, place, member, slot).wait_recv()
    mine = hid[member].reshape(-1, hid.shape[-1])
    units = hid.shape[-1]
    for slot in range(GROUP):
        theirs = hid[slot].reshape(-1, units)
        gram[:, slot * units:(slot + 1) * units] = lax.dot_general(
            mine, theirs, (((0,), (0,)), ((), ())), preferred_element_type=F32
        ) * (1.0 / (fronts * CAP))
    store_gram = pltpu.make_async_copy(gram, hess.at[0], hess_sem)
    store_gram.start()

    stage_e(fronts - 1)

    @pl.when(layer > 0)
    def _():
        copy_routes(layer - 1).wait_send()

    def finish(f, carry):
        for step in range(1, RING):
            copy_b(f, at_x(step), x).wait_send()
            copy_d(f, at_x(step), x).wait_send()
        for to_place, to_member in group:
            copy_h(f, to_place, to_member, member).wait_send()
        for step in range(1, PLANES):
            copy_e(f, at_z(step), z).wait_send()

        @pl.when(is_first)
        def _():
            for step in range(1, PLANES):
                copy_s(f, at_z(step)).wait_send()

        @pl.when(layer < sections - 1)
        def _():
            for step in range(PLANES):
                copy_a(f, at_z(step), z, layer + 1).wait_send()
            copy_x(f, layer + 1).wait_send()

        store_out(f).wait()
        return carry

    lax.fori_loop(0, fronts, finish, 0)
    store_gram.wait()


def shards(stream_in, gain, w_gate, w_up, w_down, routes, gates):
    fronts, tokens, width = stream_in.shape
    units = w_gate.shape[2]
    slots = PLANES * CAP
    flight = PLANES // 2
    dma = pltpu.SemaphoreType.DMA
    anywhere = pl.BlockSpec(memory_space=pl.ANY)
    vmem = pl.BlockSpec(memory_space=pltpu.VMEM)
    route_cols = jnp.swapaxes(routes[0], 1, 2)
    gate_cols = jnp.swapaxes(gates[0], 1, 2)
    return pl.pallas_call(
        kernel,
        out_shape=(
            jax.ShapeDtypeStruct((1, fronts, tokens, width), BF16),
            jax.ShapeDtypeStruct((1, units, GROUP * units), F32),
        ),
        in_specs=[anywhere, vmem, anywhere, anywhere, anywhere, vmem, vmem],
        out_specs=(anywhere, anywhere),
        scratch_shapes=[
            pltpu.VMEM((width, units), BF16),
            pltpu.VMEM((width, units), BF16),
            pltpu.VMEM((units, width), BF16),
            pltpu.VMEM(route_cols.shape, jnp.int32),
            pltpu.VMEM((fronts, flight * CAP, tokens), BF16),
            pltpu.VMEM((fronts, tokens, tokens + 2 * slots), BF16),
            pltpu.VMEM((fronts, flight * CAP, tokens + 2 * slots), BF16),
            pltpu.VMEM((fronts, tokens, width), BF16),
            pltpu.VMEM((fronts, tokens, width), BF16),
            pltpu.VMEM((fronts, flight, CAP, width), BF16),
            pltpu.VMEM((fronts, flight, CAP, width), BF16),
            pltpu.VMEM((fronts, PLANES, CAP, width), BF16),
            pltpu.VMEM((fronts, RING, slots, width), BF16),
            pltpu.VMEM((fronts, RING, slots, width), BF16),
            pltpu.VMEM((fronts, RING, slots, width), BF16),
            pltpu.VMEM((fronts, PLANES, CAP, width), BF16),
            pltpu.VMEM((fronts, PLANES, CAP, width), BF16),
            pltpu.VMEM((GROUP, fronts, RING * slots, units), BF16),
            pltpu.VMEM((units, GROUP * units), F32),
            dma((3,)), dma((fronts,)), dma((fronts,)), dma,
            dma, dma,
            dma((fronts, PLANES)),
            dma((fronts, PLANES)), dma((fronts, PLANES)),
            dma((fronts, RING)), dma((fronts, RING)),
            dma((fronts, GROUP)), dma((fronts, GROUP)),
            dma((fronts, RING)), dma((fronts, RING)),
            dma((fronts, PLANES)), dma((fronts, PLANES)),
            dma((fronts,)), dma((fronts,)),
        ],
        compiler_params=pltpu.CompilerParams(
            collective_id=0, has_side_effects=True, vmem_limit_bytes=48 * 1024 * 1024
        ),
    )(stream_in, gain, w_gate, w_up, w_down, route_cols, gate_cols)


def solution(mesh):
    return jax.shard_map(
        shards,
        mesh=mesh,
        in_specs=(
            P(None, "expert", None),
            P("layer", None),
            P("layer", None, "expert"),
            P("layer", None, "expert"),
            P("layer", "expert", None),
            P("layer", None, "expert", None),
            P("layer", None, "expert", None),
        ),
        out_specs=(P("layer", None, "expert", None), P("layer", "expert", None)),
        check_vma=False,
    )
```

```python
import functools

import jax
import jax.numpy as jnp
from jax import lax
from jax.experimental import pallas as pl
from jax.experimental.pallas import tpu as pltpu
from jax.sharding import PartitionSpec as P

GROUP = 8
CAP = 2
EPSILON = 1e-06
MESH = pl.DeviceIdType.MESH
PLANES = 8
RING = 4
CHUNKS = 4
BF16 = jnp.bfloat16
F32 = jnp.float32


def first_and_second(route, expert, lanes):
    routed = jnp.max((route == expert).astype(F32), axis=0, keepdims=True)
    first = jnp.min(jnp.where(routed > 0, lanes, 1000), axis=1, keepdims=True)
    slot0 = jnp.where(lanes == first, routed, 0.0)
    return slot0, routed - slot0


def kernel(
    stream, gain, wg, wu, wd, routes, gates,
    out, hess,
    wg_v, wu_v, wd_v, routes_next,
    pick_own, mix_full, mix_next,
    xin, xout, sbuf, abuf, arecv, scales, rows, part, drecv, ebuf, erecv, hid, gram,
    w_sem, in_sem, out_sem, hess_sem,
    r_send, r_recv, s_send, a_send, a_recv, b_send, b_recv, c_send, c_recv,
    h_send, h_recv, d_send, d_recv, e_send, e_recv, x_send, x_recv,
):
    fronts, tokens, width = xin.shape
    chunks, part_width = sbuf.shape[1], sbuf.shape[-1]
    flight = PLANES // 2
    sections = lax.axis_size("layer")
    layer = lax.axis_index("layer")
    place = lax.axis_index("expert")
    z, x = place // RING, place % RING
    half = z % 2
    member = half * RING + x
    is_first, is_last = layer == 0, layer == sections - 1

    def at_z(step):
        return lax.rem(z + step, PLANES)

    def at_x(step):
        return lax.rem(x + step, RING)

    def peers():
        group = []
        for other in (0, 1):
            for step in range(RING):
                if other or step:
                    p = lax.rem(half + other, 2)
                    nx = at_x(step)
                    group.append(((z - half + p) * RING + nx, p * RING + nx))
        return group

    group = peers()

    def remote(src, dst, send, recv, to_layer, to_place):
        return pltpu.make_async_remote_copy(
            src_ref=src, dst_ref=dst, send_sem=send, recv_sem=recv,
            device_id=(to_layer, to_place), device_id_type=MESH,
        )

    def copy_routes(to_layer):
        return remote(routes, routes_next, r_send, r_recv, to_layer, place)

    def copy_s(f, c, to_z):
        return remote(sbuf.at[f, c, to_z // 2], arecv.at[f, c, z],
                      s_send.at[f, c, to_z], a_recv.at[f, c, z], layer, to_z * RING + x)

    def copy_a(f, c, to_z, slot, to_layer):
        return remote(abuf.at[f, c, to_z // 2], arecv.at[f, c, slot],
                      a_send.at[f, c, to_z], a_recv.at[f, c, slot], to_layer, to_z * RING + x)

    def copy_b(f, c, to_x, slot):
        return remote(rows.at[f, c, slot], rows.at[f, c, slot],
                      b_send.at[f, c, to_x], b_recv.at[f, c, slot], layer, z * RING + to_x)

    def copy_c(f, to_x, slot):
        return remote(scales.at[f, slot], scales.at[f, slot],
                      c_send.at[f, to_x], c_recv.at[f, slot], layer, z * RING + to_x)

    def copy_h(f, to_place, to_member, slot):
        return remote(hid.at[slot, f], hid.at[slot, f], h_send.at[f, to_member], h_recv.at[f, slot],
                      layer, to_place)

    def copy_d(f, c, to_x, slot):
        return remote(part.at[f, c, to_x], drecv.at[f, c, slot],
                      d_send.at[f, c, to_x], d_recv.at[f, c, slot], layer, z * RING + to_x)

    def copy_e(f, c, to_z, slot):
        return remote(ebuf.at[f, c, to_z], erecv.at[f, c, slot],
                      e_send.at[f, c, to_z], e_recv.at[f, c, slot], layer, to_z * RING + x)

    def columns(c):
        return slice(c * part_width, (c + 1) * part_width)

    def copy_x(f, to_layer):
        return remote(xout.at[f], xin.at[f], x_send.at[f], x_recv.at[f], to_layer, place)

    def load_stream(f):
        return pltpu.make_async_copy(stream.at[f], xin.at[f], in_sem.at[f])

    def store_out(f):
        return pltpu.make_async_copy(xout.at[f], out.at[0, f], out_sem.at[f])

    weights = (
        pltpu.make_async_copy(wg.at[0], wg_v, w_sem.at[0]),
        pltpu.make_async_copy(wu.at[0], wu_v, w_sem.at[1]),
        pltpu.make_async_copy(wd.at[0], wd_v, w_sem.at[2]),
    )

    @pl.when(is_first)
    def _():
        for f in range(fronts):
            load_stream(f).start()

    for load in weights:
        load.start()

    barrier = pltpu.get_barrier_semaphore()

    def greet(to_layer, to_place):
        pl.semaphore_signal(barrier, inc=1, device_id=(to_layer, to_place), device_id_type=MESH)

    @pl.when(layer > 0)
    def _():
        for step in range(PLANES):
            greet(layer - 1, at_z(step) * RING + x)

    @pl.when(layer < sections - 1)
    def _():
        greet(layer + 1, place)

    for step in range(1, PLANES):
        greet(layer, at_z(step) * RING + x)
    for step in range(1, RING):
        greet(layer, z * RING + at_x(step))
    for step in range(1, RING):
        greet(layer, (z - half + (1 - half)) * RING + at_x(step))

    lanes = lax.broadcasted_iota(jnp.int32, (1, tokens), 1)
    row8 = lax.broadcasted_iota(jnp.int32, (flight * CAP, tokens), 0)
    row16 = lax.broadcasted_iota(jnp.int32, (2 * flight * CAP, tokens), 0)
    eye = (
        lax.broadcasted_iota(jnp.int32, (tokens, tokens), 0)
        == lax.broadcasted_iota(jnp.int32, (tokens, tokens), 1)
    ).astype(BF16)

    def own_tables(f):
        route, gate = routes[f], gates[f]
        pick = jnp.zeros((flight * CAP, tokens), F32)
        scaled = jnp.zeros((2 * flight * CAP, tokens), F32)
        for expert in range(flight):
            slots = first_and_second(route, expert, lanes)
            weight = jnp.sum(jnp.where(route == expert, gate, 0.0), axis=0, keepdims=True)
            for c in range(CAP):
                pick = jnp.where(row8 == expert * CAP + c, slots[c], pick)
                here = jnp.logical_and(row16 // (2 * CAP) == expert, row16 % CAP == c)
                scaled = jnp.where(here, slots[c] * weight, scaled)
        pick_own[f] = pick.astype(BF16)
        mix = scaled.T
        high = mix.astype(BF16)
        low = (mix - high.astype(F32)).astype(BF16)
        mix_full[f] = jnp.concatenate([eye, high, low], axis=1)

    def next_tables(f):
        route = routes_next[f]
        pick = jnp.zeros((flight * CAP, tokens), F32)
        for expert in range(flight):
            slots = first_and_second(route, expert, lanes)
            for c in range(CAP):
                pick = jnp.where(row8 == expert * CAP + c, slots[c], pick)
        mix_next[f] = jnp.dot(
            pick.astype(BF16), mix_full[f], preferred_element_type=F32
        ).astype(BF16)

    for f in range(fronts):
        own_tables(f)

    @pl.when(jnp.logical_and(is_first, is_last))
    def _():
        pl.semaphore_wait(barrier, 13)

    @pl.when(jnp.logical_and(is_first, jnp.logical_not(is_last)))
    def _():
        pl.semaphore_wait(barrier, 13 + PLANES)

    @pl.when(jnp.logical_and(jnp.logical_not(is_first), is_last))
    def _():
        pl.semaphore_wait(barrier, 13 + 1)

    @pl.when(jnp.logical_and(jnp.logical_not(is_first), jnp.logical_not(is_last)))
    def _():
        pl.semaphore_wait(barrier, 13 + 1 + PLANES)

    @pl.when(layer > 0)
    def _():
        copy_routes(layer - 1).start()

    def stage_s(f):
        load_stream(f).wait()
        for c in range(chunks):
            picked = jnp.dot(pick_own[f], xin[f, :, columns(c)], preferred_element_type=F32)
            sbuf[f, c] = picked.astype(BF16).reshape(flight, CAP, part_width)
            for step in range(1, PLANES):
                copy_s(f, c, at_z(step)).start()
            arecv[f, c, z] = sbuf[f, c, z // 2]

    def stage_a(f):
        squares = jnp.zeros((PLANES * CAP, 1), F32)
        for c in range(chunks):
            for step in range(1, PLANES):
                copy_a(f, c, z, at_z(step), layer).wait_recv()

            @pl.when(layer > 0)
            def _():
                copy_a(f, c, z, z, layer).wait_recv()

            wide = arecv[f, c].reshape(PLANES * CAP, part_width).astype(F32)
            rows[f, c, x] = (wide * gain[:, columns(c)]).astype(BF16)
            for step in (2, 1, 3):
                copy_b(f, c, at_x(step), x).start()
            squares = squares + jnp.sum(wide * wide, axis=-1, keepdims=True)
        scale = lax.rsqrt(squares * (1.0 / width) + EPSILON)
        scales[f, x] = jnp.broadcast_to(scale, scales.shape[2:])
        for step in (2, 1, 3):
            copy_c(f, at_x(step), x).start()

    def stage_b(f):
        count = RING * PLANES * CAP
        gate_act = jnp.zeros((count, wg_v.shape[1]), F32)
        up_act = jnp.zeros((count, wg_v.shape[1]), F32)
        for c in range(chunks):
            for step in range(1, RING):
                copy_b(f, c, x, at_x(step)).wait_recv()
            all_rows = rows[f, c].reshape(count, part_width)
            gate_act += jnp.dot(all_rows, wg_v[columns(c), :], preferred_element_type=F32)
            up_act += jnp.dot(all_rows, wu_v[columns(c), :], preferred_element_type=F32)
        for step in range(1, RING):
            copy_c(f, x, at_x(step)).wait_recv()
        scale = scales[f].reshape(count, scales.shape[-1])[:, :1]
        hidden = (jax.nn.silu(gate_act * scale) * (up_act * scale)).astype(BF16)
        for c in range(chunks):
            partial = jnp.dot(hidden, wd_v[:, columns(c)], preferred_element_type=F32)
            part[f, c] = partial.astype(BF16).reshape(RING, PLANES * CAP, part_width)
            for step in (2, 1, 3):
                copy_d(f, c, at_x(step), x).start()
        hid[member, f] = hidden
        for to_place, to_member in group:
            copy_h(f, to_place, to_member, member).start()

    def stage_d(f):
        for c in range(chunks):
            for step in range(1, RING):
                copy_d(f, c, x, at_x(step)).wait_recv()
            total = part[f, c, x].astype(F32)
            for step in range(1, RING):
                total = total + drecv[f, c, at_x(step)].astype(F32)
            ebuf[f, c] = total.astype(BF16).reshape(PLANES, CAP, part_width)
            for step in range(1, PLANES):
                copy_e(f, c, at_z(step), z).start()
            erecv[f, c, z] = ebuf[f, c, z]

    def stage_e(f):
        @pl.when(layer > 0)
        def _():
            copy_x(f, layer).wait_recv()

        def stack(c):
            returned = erecv[f, c].reshape(PLANES * CAP, part_width)
            return jnp.concatenate([xin[f, :, columns(c)], returned, returned], axis=0)

        for c in range(chunks):
            for step in range(1, PLANES):
                copy_e(f, c, z, at_z(step)).wait_recv()

            @pl.when(layer < sections - 1)
            def _():
                picked = jnp.dot(mix_next[f], stack(c), preferred_element_type=F32)
                abuf[f, c] = picked.astype(BF16).reshape(flight, CAP, part_width)
                for step in range(PLANES):
                    copy_a(f, c, at_z(step), z, layer + 1).start()

        for c in range(chunks):
            xout[f, :, columns(c)] = jnp.dot(
                mix_full[f], stack(c), preferred_element_type=F32
            ).astype(BF16)

        @pl.when(layer < sections - 1)
        def _():
            copy_x(f, layer + 1).start()

        store_out(f).start()

    @pl.when(is_first)
    def _():
        stage_s(0)

    @pl.when(layer < sections - 1)
    def _():
        copy_routes(layer).wait_recv()
        for f in range(fronts):
            next_tables(f)

    for load in weights:
        load.wait()

    stage_a(0)

    stage_b(0)

    def steady(f, carry):

        @pl.when(is_first)
        def _():
            stage_s(f + 1)

        stage_d(f)
        stage_a(f + 1)
        stage_e(f)
        stage_b(f + 1)
        return carry

    lax.fori_loop(0, fronts - 1, steady, 0)
    stage_d(fronts - 1)

    for f in range(fronts):
        for _, slot in group:
            copy_h(f, place, member, slot).wait_recv()
    mine = hid[member].reshape(-1, hid.shape[-1])
    units = hid.shape[-1]
    for slot in range(GROUP):
        theirs = hid[slot].reshape(-1, units)
        gram[:, slot * units:(slot + 1) * units] = lax.dot_general(
            mine, theirs, (((0,), (0,)), ((), ())), preferred_element_type=F32
        ) * (1.0 / (fronts * CAP))
    store_gram = pltpu.make_async_copy(gram, hess.at[0], hess_sem)
    store_gram.start()

    stage_e(fronts - 1)

    @pl.when(layer > 0)
    def _():
        copy_routes(layer - 1).wait_send()

    def finish(f, carry):
        for step in range(1, RING):
            copy_c(f, at_x(step), x).wait_send()
        for to_place, to_member in group:
            copy_h(f, to_place, to_member, member).wait_send()
        for c in range(chunks):
            for step in range(1, RING):
                copy_b(f, c, at_x(step), x).wait_send()
                copy_d(f, c, at_x(step), x).wait_send()
            for step in range(1, PLANES):
                copy_e(f, c, at_z(step), z).wait_send()

        @pl.when(is_first)
        def _():
            for c in range(chunks):
                for step in range(1, PLANES):
                    copy_s(f, c, at_z(step)).wait_send()

        @pl.when(layer < sections - 1)
        def _():
            for c in range(chunks):
                for step in range(PLANES):
                    copy_a(f, c, at_z(step), z, layer + 1).wait_send()
            copy_x(f, layer + 1).wait_send()

        store_out(f).wait()
        return carry

    lax.fori_loop(0, fronts, finish, 0)
    store_gram.wait()


def shards(stream_in, gain, w_gate, w_up, w_down, routes, gates):
    fronts, tokens, width = stream_in.shape
    units = w_gate.shape[2]
    slots = PLANES * CAP
    flight = PLANES // 2
    part_width = width // CHUNKS
    dma = pltpu.SemaphoreType.DMA
    anywhere = pl.BlockSpec(memory_space=pl.ANY)
    vmem = pl.BlockSpec(memory_space=pltpu.VMEM)
    route_cols = jnp.swapaxes(routes[0], 1, 2)
    gate_cols = jnp.swapaxes(gates[0], 1, 2)
    return pl.pallas_call(
        kernel,
        out_shape=(
            jax.ShapeDtypeStruct((1, fronts, tokens, width), BF16),
            jax.ShapeDtypeStruct((1, units, GROUP * units), F32),
        ),
        in_specs=[anywhere, vmem, anywhere, anywhere, anywhere, vmem, vmem],
        out_specs=(anywhere, anywhere),
        scratch_shapes=[
            pltpu.VMEM((width, units), BF16),
            pltpu.VMEM((width, units), BF16),
            pltpu.VMEM((units, width), BF16),
            pltpu.VMEM(route_cols.shape, jnp.int32),
            pltpu.VMEM((fronts, flight * CAP, tokens), BF16),
            pltpu.VMEM((fronts, tokens, tokens + 2 * slots), BF16),
            pltpu.VMEM((fronts, flight * CAP, tokens + 2 * slots), BF16),
            pltpu.VMEM((fronts, tokens, width), BF16),
            pltpu.VMEM((fronts, tokens, width), BF16),
            pltpu.VMEM((fronts, CHUNKS, flight, CAP, part_width), BF16),
            pltpu.VMEM((fronts, CHUNKS, flight, CAP, part_width), BF16),
            pltpu.VMEM((fronts, CHUNKS, PLANES, CAP, part_width), BF16),
            pltpu.VMEM((fronts, RING, slots, 128), F32),
            pltpu.VMEM((fronts, CHUNKS, RING, slots, part_width), BF16),
            pltpu.VMEM((fronts, CHUNKS, RING, slots, part_width), BF16),
            pltpu.VMEM((fronts, CHUNKS, RING, slots, part_width), BF16),
            pltpu.VMEM((fronts, CHUNKS, PLANES, CAP, part_width), BF16),
            pltpu.VMEM((fronts, CHUNKS, PLANES, CAP, part_width), BF16),
            pltpu.VMEM((GROUP, fronts, RING * slots, units), BF16),
            pltpu.VMEM((units, GROUP * units), F32),
            dma((3,)), dma((fronts,)), dma((fronts,)), dma,
            dma, dma,
            dma((fronts, CHUNKS, PLANES)),
            dma((fronts, CHUNKS, PLANES)), dma((fronts, CHUNKS, PLANES)),
            dma((fronts, CHUNKS, RING)), dma((fronts, CHUNKS, RING)),
            dma((fronts, RING)), dma((fronts, RING)),
            dma((fronts, GROUP)), dma((fronts, GROUP)),
            dma((fronts, CHUNKS, RING)), dma((fronts, CHUNKS, RING)),
            dma((fronts, CHUNKS, PLANES)), dma((fronts, CHUNKS, PLANES)),
            dma((fronts,)), dma((fronts,)),
        ],
        compiler_params=pltpu.CompilerParams(
            collective_id=0, has_side_effects=True, vmem_limit_bytes=60 * 1024 * 1024
        ),
    )(stream_in, gain, w_gate, w_up, w_down, route_cols, gate_cols)


def solution(mesh):
    return jax.shard_map(
        shards,
        mesh=mesh,
        in_specs=(
            P(None, "expert", None),
            P("layer", None),
            P("layer", None, "expert"),
            P("layer", None, "expert"),
            P("layer", "expert", None),
            P("layer", None, "expert", None),
            P("layer", None, "expert", None),
        ),
        out_specs=(P("layer", None, "expert", None), P("layer", "expert", None)),
        check_vma=False,
    )
```

```python
import functools

import jax
import jax.numpy as jnp
from jax import lax
from jax.experimental import pallas as pl
from jax.experimental.pallas import tpu as pltpu
from jax.sharding import PartitionSpec as P

GROUP = 8
CAP = 2
EPSILON = 1e-06
MESH = pl.DeviceIdType.MESH
PLANES = 8
RING = 4
CHUNKS = 4
BF16 = jnp.bfloat16
F32 = jnp.float32


def first_and_second(route, expert, lanes):
    routed = jnp.max((route == expert).astype(F32), axis=0, keepdims=True)
    first = jnp.min(jnp.where(routed > 0, lanes, 1000), axis=1, keepdims=True)
    slot0 = jnp.where(lanes == first, routed, 0.0)
    return slot0, routed - slot0


def kernel(
    stream, gain, wg, wu, wd, routes, gates,
    out, hess,
    wg_v, wu_v, wd_v, routes_next,
    pick_own, mix_full, mix_next,
    xin, xout, sbuf, abuf, arecv, scales, rows, part, drecv, ebuf, erecv, hid, gram,
    w_sem, in_sem, out_sem, hess_sem,
    r_send, r_recv, s_send, a_send, a_recv, b_send, b_recv, c_send, c_recv,
    h_send, h_recv, d_send, d_recv, e_send, e_recv, x_send, x_recv,
):
    fronts, tokens, width = xin.shape
    chunks, part_width = sbuf.shape[1], sbuf.shape[-1]
    flight = PLANES // 2
    sections = lax.axis_size("layer")
    layer = lax.axis_index("layer")
    place = lax.axis_index("expert")
    z, x = place // RING, place % RING
    half = z % 2
    member = half * RING + x
    is_first, is_last = layer == 0, layer == sections - 1

    def at_z(step):
        return lax.rem(z + step, PLANES)

    def at_x(step):
        return lax.rem(x + step, RING)

    opposite = (z - half + (1 - half)) * RING + x

    def remote(src, dst, send, recv, to_layer, to_place):
        return pltpu.make_async_remote_copy(
            src_ref=src, dst_ref=dst, send_sem=send, recv_sem=recv,
            device_id=(to_layer, to_place), device_id_type=MESH,
        )

    def copy_routes(to_layer):
        return remote(routes, routes_next, r_send, r_recv, to_layer, place)

    def copy_s(f, c, to_z):
        return remote(sbuf.at[f, c, to_z // 2], arecv.at[f, c, z],
                      s_send.at[f, c, to_z], a_recv.at[f, c, z], layer, to_z * RING + x)

    def copy_a(f, c, to_z, slot, to_layer):
        return remote(abuf.at[f, c, to_z // 2], arecv.at[f, c, slot],
                      a_send.at[f, c, to_z], a_recv.at[f, c, slot], to_layer, to_z * RING + x)

    def copy_b(f, c, to_x, slot):
        return remote(rows.at[f, c, slot], rows.at[f, c, slot],
                      b_send.at[f, c, to_x], b_recv.at[f, c, slot], layer, z * RING + to_x)

    def copy_c(f, to_x, slot):
        return remote(scales.at[f, slot], scales.at[f, slot],
                      c_send.at[f, to_x], c_recv.at[f, slot], layer, z * RING + to_x)

    def copy_h(f, to_place, slot, number):
        return remote(hid.at[slot, f], hid.at[slot, f], h_send.at[f, number], h_recv.at[f, slot],
                      layer, to_place)

    def copy_d(f, c, to_x, slot):
        return remote(part.at[f, c, to_x], drecv.at[f, c, slot],
                      d_send.at[f, c, to_x], d_recv.at[f, c, slot], layer, z * RING + to_x)

    def copy_e(f, c, to_z, slot):
        return remote(ebuf.at[f, c, to_z], erecv.at[f, c, slot],
                      e_send.at[f, c, to_z], e_recv.at[f, c, slot], layer, to_z * RING + x)

    def columns(c):
        return slice(c * part_width, (c + 1) * part_width)

    def copy_x(f, to_layer):
        return remote(xout.at[f], xin.at[f], x_send.at[f], x_recv.at[f], to_layer, place)

    def load_stream(f):
        return pltpu.make_async_copy(stream.at[f], xin.at[f], in_sem.at[f])

    def store_out(f):
        return pltpu.make_async_copy(xout.at[f], out.at[0, f], out_sem.at[f])

    weights = (
        pltpu.make_async_copy(wg.at[0], wg_v, w_sem.at[0]),
        pltpu.make_async_copy(wu.at[0], wu_v, w_sem.at[1]),
        pltpu.make_async_copy(wd.at[0], wd_v, w_sem.at[2]),
    )

    @pl.when(is_first)
    def _():
        for f in range(fronts):
            load_stream(f).start()

    for load in weights:
        load.start()

    barrier = pltpu.get_barrier_semaphore()

    def greet(to_layer, to_place):
        pl.semaphore_signal(barrier, inc=1, device_id=(to_layer, to_place), device_id_type=MESH)

    @pl.when(layer > 0)
    def _():
        for step in range(PLANES):
            greet(layer - 1, at_z(step) * RING + x)

    @pl.when(layer < sections - 1)
    def _():
        greet(layer + 1, place)

    for step in range(1, PLANES):
        greet(layer, at_z(step) * RING + x)
    for step in range(1, RING):
        greet(layer, z * RING + at_x(step))

    lanes = lax.broadcasted_iota(jnp.int32, (1, tokens), 1)
    row8 = lax.broadcasted_iota(jnp.int32, (flight * CAP, tokens), 0)
    row16 = lax.broadcasted_iota(jnp.int32, (2 * flight * CAP, tokens), 0)
    eye = (
        lax.broadcasted_iota(jnp.int32, (tokens, tokens), 0)
        == lax.broadcasted_iota(jnp.int32, (tokens, tokens), 1)
    ).astype(BF16)

    def own_tables(f):
        route, gate = routes[f], gates[f]
        pick = jnp.zeros((flight * CAP, tokens), F32)
        scaled = jnp.zeros((2 * flight * CAP, tokens), F32)
        for expert in range(flight):
            slots = first_and_second(route, expert, lanes)
            weight = jnp.sum(jnp.where(route == expert, gate, 0.0), axis=0, keepdims=True)
            for c in range(CAP):
                pick = jnp.where(row8 == expert * CAP + c, slots[c], pick)
                here = jnp.logical_and(row16 // (2 * CAP) == expert, row16 % CAP == c)
                scaled = jnp.where(here, slots[c] * weight, scaled)
        pick_own[f] = pick.astype(BF16)
        mix = scaled.T
        high = mix.astype(BF16)
        low = (mix - high.astype(F32)).astype(BF16)
        mix_full[f] = jnp.concatenate([eye, high, low], axis=1)

    def next_tables(f):
        route = routes_next[f]
        pick = jnp.zeros((flight * CAP, tokens), F32)
        for expert in range(flight):
            slots = first_and_second(route, expert, lanes)
            for c in range(CAP):
                pick = jnp.where(row8 == expert * CAP + c, slots[c], pick)
        mix_next[f] = jnp.dot(
            pick.astype(BF16), mix_full[f], preferred_element_type=F32
        ).astype(BF16)

    for f in range(fronts):
        own_tables(f)

    @pl.when(jnp.logical_and(is_first, is_last))
    def _():
        pl.semaphore_wait(barrier, 10)

    @pl.when(jnp.logical_and(is_first, jnp.logical_not(is_last)))
    def _():
        pl.semaphore_wait(barrier, 10 + PLANES)

    @pl.when(jnp.logical_and(jnp.logical_not(is_first), is_last))
    def _():
        pl.semaphore_wait(barrier, 10 + 1)

    @pl.when(jnp.logical_and(jnp.logical_not(is_first), jnp.logical_not(is_last)))
    def _():
        pl.semaphore_wait(barrier, 10 + 1 + PLANES)

    @pl.when(layer > 0)
    def _():
        copy_routes(layer - 1).start()

    def stage_s(f):
        load_stream(f).wait()
        for c in range(chunks):
            picked = jnp.dot(pick_own[f], xin[f, :, columns(c)], preferred_element_type=F32)
            sbuf[f, c] = picked.astype(BF16).reshape(flight, CAP, part_width)
            for step in range(1, PLANES):
                copy_s(f, c, at_z(step)).start()
            arecv[f, c, z] = sbuf[f, c, z // 2]

    def stage_a(f):
        squares = jnp.zeros((PLANES * CAP, 1), F32)
        for c in range(chunks):
            for step in range(1, PLANES):
                copy_a(f, c, z, at_z(step), layer).wait_recv()

            @pl.when(layer > 0)
            def _():
                copy_a(f, c, z, z, layer).wait_recv()

            wide = arecv[f, c].reshape(PLANES * CAP, part_width).astype(F32)
            rows[f, c, x] = (wide * gain[:, columns(c)]).astype(BF16)
            for step in (2, 1, 3):
                copy_b(f, c, at_x(step), x).start()
            squares = squares + jnp.sum(wide * wide, axis=-1, keepdims=True)
        scale = lax.rsqrt(squares * (1.0 / width) + EPSILON)
        scales[f, x] = jnp.broadcast_to(scale, scales.shape[2:])
        for step in (2, 1, 3):
            copy_c(f, at_x(step), x).start()

    def stage_b(f):
        count = RING * PLANES * CAP
        gate_act = jnp.zeros((count, wg_v.shape[1]), F32)
        up_act = jnp.zeros((count, wg_v.shape[1]), F32)
        for c in range(chunks):
            for step in range(1, RING):
                copy_b(f, c, x, at_x(step)).wait_recv()
            all_rows = rows[f, c].reshape(count, part_width)
            gate_act += jnp.dot(all_rows, wg_v[columns(c), :], preferred_element_type=F32)
            up_act += jnp.dot(all_rows, wu_v[columns(c), :], preferred_element_type=F32)
        for step in range(1, RING):
            copy_c(f, x, at_x(step)).wait_recv()
        scale = scales[f].reshape(count, scales.shape[-1])[:, :1]
        hidden = (jax.nn.silu(gate_act * scale) * (up_act * scale)).astype(BF16)
        for c in range(chunks):
            partial = jnp.dot(hidden, wd_v[:, columns(c)], preferred_element_type=F32)
            part[f, c] = partial.astype(BF16).reshape(RING, PLANES * CAP, part_width)
            for step in (2, 1, 3):
                copy_d(f, c, at_x(step), x).start()
        hid[member, f] = hidden
        copy_h(f, opposite, member, PLANES).start()
        for step in (2, 1, 3):
            copy_h(f, z * RING + at_x(step), half * RING + x, at_x(step)).start()

    def stage_h(f):
        for step in range(1, RING):
            slot = half * RING + at_x(step)
            copy_h(f, place, slot, PLANES).wait_recv()
            copy_h(f, opposite, slot, PLANES + step).start()

    def stage_d(f):
        for c in range(chunks):
            for step in range(1, RING):
                copy_d(f, c, x, at_x(step)).wait_recv()
            total = part[f, c, x].astype(F32)
            for step in range(1, RING):
                total = total + drecv[f, c, at_x(step)].astype(F32)
            ebuf[f, c] = total.astype(BF16).reshape(PLANES, CAP, part_width)
            for step in range(1, PLANES):
                copy_e(f, c, at_z(step), z).start()
            erecv[f, c, z] = ebuf[f, c, z]

    def stage_e(f):
        @pl.when(layer > 0)
        def _():
            copy_x(f, layer).wait_recv()

        def stack(c):
            returned = erecv[f, c].reshape(PLANES * CAP, part_width)
            return jnp.concatenate([xin[f, :, columns(c)], returned, returned], axis=0)

        for c in range(chunks):
            for step in range(1, PLANES):
                copy_e(f, c, z, at_z(step)).wait_recv()

            @pl.when(layer < sections - 1)
            def _():
                picked = jnp.dot(mix_next[f], stack(c), preferred_element_type=F32)
                abuf[f, c] = picked.astype(BF16).reshape(flight, CAP, part_width)
                for step in range(PLANES):
                    copy_a(f, c, at_z(step), z, layer + 1).start()

        for c in range(chunks):
            xout[f, :, columns(c)] = jnp.dot(
                mix_full[f], stack(c), preferred_element_type=F32
            ).astype(BF16)

        @pl.when(layer < sections - 1)
        def _():
            copy_x(f, layer + 1).start()

        store_out(f).start()

    @pl.when(is_first)
    def _():
        stage_s(0)

    @pl.when(layer < sections - 1)
    def _():
        copy_routes(layer).wait_recv()
        for f in range(fronts):
            next_tables(f)

    for load in weights:
        load.wait()

    stage_a(0)

    stage_b(0)

    def steady(f, carry):

        @pl.when(is_first)
        def _():
            stage_s(f + 1)

        stage_d(f)
        stage_a(f + 1)
        stage_e(f)
        stage_h(f)
        stage_b(f + 1)
        return carry

    lax.fori_loop(0, fronts - 1, steady, 0)
    store_gram = pltpu.make_async_copy(gram, hess.at[0], hess_sem)

    def stage_gram():
        for f in range(fronts):
            for column in range(RING):
                copy_h(f, place, (1 - half) * RING + column, PLANES).wait_recv()
        mine = hid[member].reshape(-1, hid.shape[-1])
        units = hid.shape[-1]
        for slot in range(GROUP):
            theirs = hid[slot].reshape(-1, units)
            gram[:, slot * units:(slot + 1) * units] = lax.dot_general(
                mine, theirs, (((0,), (0,)), ((), ())), preferred_element_type=F32
            ) * (1.0 / (fronts * CAP))
        store_gram.start()

    last = fronts - 1
    stage_d(last)
    stage_h(last)
    stage_e(last)
    stage_gram()

    @pl.when(layer > 0)
    def _():
        copy_routes(layer - 1).wait_send()

    def finish(f, carry):
        for step in range(1, RING):
            copy_c(f, at_x(step), x).wait_send()
        copy_h(f, opposite, member, PLANES).wait_send()
        for step in range(1, RING):
            copy_h(f, place, member, at_x(step)).wait_send()
            copy_h(f, opposite, member, PLANES + step).wait_send()
        for c in range(chunks):
            for step in range(1, RING):
                copy_b(f, c, at_x(step), x).wait_send()
                copy_d(f, c, at_x(step), x).wait_send()
            for step in range(1, PLANES):
                copy_e(f, c, at_z(step), z).wait_send()

        @pl.when(is_first)
        def _():
            for c in range(chunks):
                for step in range(1, PLANES):
                    copy_s(f, c, at_z(step)).wait_send()

        @pl.when(layer < sections - 1)
        def _():
            for c in range(chunks):
                for step in range(PLANES):
                    copy_a(f, c, at_z(step), z, layer + 1).wait_send()
            copy_x(f, layer + 1).wait_send()

        store_out(f).wait()
        return carry

    lax.fori_loop(0, fronts, finish, 0)
    store_gram.wait()


def shards(stream_in, gain, w_gate, w_up, w_down, routes, gates):
    fronts, tokens, width = stream_in.shape
    units = w_gate.shape[2]
    slots = PLANES * CAP
    flight = PLANES // 2
    part_width = width // CHUNKS
    dma = pltpu.SemaphoreType.DMA
    anywhere = pl.BlockSpec(memory_space=pl.ANY)
    vmem = pl.BlockSpec(memory_space=pltpu.VMEM)
    route_cols = jnp.swapaxes(routes[0], 1, 2)
    gate_cols = jnp.swapaxes(gates[0], 1, 2)
    return pl.pallas_call(
        kernel,
        out_shape=(
            jax.ShapeDtypeStruct((1, fronts, tokens, width), BF16),
            jax.ShapeDtypeStruct((1, units, GROUP * units), F32),
        ),
        in_specs=[anywhere, vmem, anywhere, anywhere, anywhere, vmem, vmem],
        out_specs=(anywhere, anywhere),
        scratch_shapes=[
            pltpu.VMEM((width, units), BF16),
            pltpu.VMEM((width, units), BF16),
            pltpu.VMEM((units, width), BF16),
            pltpu.VMEM(route_cols.shape, jnp.int32),
            pltpu.VMEM((fronts, flight * CAP, tokens), BF16),
            pltpu.VMEM((fronts, tokens, tokens + 2 * slots), BF16),
            pltpu.VMEM((fronts, flight * CAP, tokens + 2 * slots), BF16),
            pltpu.VMEM((fronts, tokens, width), BF16),
            pltpu.VMEM((fronts, tokens, width), BF16),
            pltpu.VMEM((fronts, CHUNKS, flight, CAP, part_width), BF16),
            pltpu.VMEM((fronts, CHUNKS, flight, CAP, part_width), BF16),
            pltpu.VMEM((fronts, CHUNKS, PLANES, CAP, part_width), BF16),
            pltpu.VMEM((fronts, RING, slots, 128), F32),
            pltpu.VMEM((fronts, CHUNKS, RING, slots, part_width), BF16),
            pltpu.VMEM((fronts, CHUNKS, RING, slots, part_width), BF16),
            pltpu.VMEM((fronts, CHUNKS, RING, slots, part_width), BF16),
            pltpu.VMEM((fronts, CHUNKS, PLANES, CAP, part_width), BF16),
            pltpu.VMEM((fronts, CHUNKS, PLANES, CAP, part_width), BF16),
            pltpu.VMEM((GROUP, fronts, RING * slots, units), BF16),
            pltpu.VMEM((units, GROUP * units), F32),
            dma((3,)), dma((fronts,)), dma((fronts,)), dma,
            dma, dma,
            dma((fronts, CHUNKS, PLANES)),
            dma((fronts, CHUNKS, PLANES)), dma((fronts, CHUNKS, PLANES)),
            dma((fronts, CHUNKS, RING)), dma((fronts, CHUNKS, RING)),
            dma((fronts, RING)), dma((fronts, RING)),
            dma((fronts, PLANES + RING)), dma((fronts, GROUP)),
            dma((fronts, CHUNKS, RING)), dma((fronts, CHUNKS, RING)),
            dma((fronts, CHUNKS, PLANES)), dma((fronts, CHUNKS, PLANES)),
            dma((fronts,)), dma((fronts,)),
        ],
        compiler_params=pltpu.CompilerParams(
            collective_id=0, has_side_effects=True, vmem_limit_bytes=60 * 1024 * 1024
        ),
    )(stream_in, gain, w_gate, w_up, w_down, route_cols, gate_cols)


def solution(mesh):
    return jax.shard_map(
        shards,
        mesh=mesh,
        in_specs=(
            P(None, "expert", None),
            P("layer", None),
            P("layer", None, "expert"),
            P("layer", None, "expert"),
            P("layer", "expert", None),
            P("layer", None, "expert", None),
            P("layer", None, "expert", None),
        ),
        out_specs=(P("layer", None, "expert", None), P("layer", "expert", None)),
        check_vma=False,
    )
```

```python
import functools

import jax
import jax.numpy as jnp
from jax import lax
from jax.experimental import pallas as pl
from jax.experimental.pallas import tpu as pltpu
from jax.sharding import PartitionSpec as P

GROUP = 8
CAP = 2
EPSILON = 1e-06
MESH = pl.DeviceIdType.MESH
PLANES = 8
RING = 4
CHUNKS = 4
BF16 = jnp.bfloat16
F32 = jnp.float32


def first_and_second(route, expert, lanes):
    routed = jnp.max((route == expert).astype(F32), axis=0, keepdims=True)
    first = jnp.min(jnp.where(routed > 0, lanes, 1000), axis=1, keepdims=True)
    slot0 = jnp.where(lanes == first, routed, 0.0)
    return slot0, routed - slot0


def kernel(
    stream, gain, wg, wu, wd, routes, gates,
    out, hess,
    wg_v, wu_v, wd_v, routes_next,
    pick_own, mix_full, mix_next,
    xin, xout, sbuf, abuf, arecv, scales, rows, part, drecv, ebuf, erecv, hid, gram,
    w_sem, in_sem, out_sem, hess_sem,
    r_send, r_recv, s_send, a_send, a_recv, b_send, b_recv, c_send, c_recv,
    h_send, h_recv, d_send, d_recv, e_send, e_recv, x_send, x_recv,
):
    fronts, tokens, width = xin.shape
    chunks, part_width = sbuf.shape[1], sbuf.shape[-1]
    flight = PLANES // 2
    sections = lax.axis_size("layer")
    layer = lax.axis_index("layer")
    place = lax.axis_index("expert")
    z, x = place // RING, place % RING
    half = z % 2
    member = half * RING + x
    is_first, is_last = layer == 0, layer == sections - 1

    def at_z(step):
        return lax.rem(z + step, PLANES)

    def at_x(step):
        return lax.rem(x + step, RING)

    opposite = (z - half + (1 - half)) * RING + x

    def remote(src, dst, send, recv, to_layer, to_place):
        return pltpu.make_async_remote_copy(
            src_ref=src, dst_ref=dst, send_sem=send, recv_sem=recv,
            device_id=(to_layer, to_place), device_id_type=MESH,
        )

    def copy_routes(to_layer):
        return remote(routes, routes_next, r_send, r_recv, to_layer, place)

    def copy_s(f, c, to_z):
        return remote(sbuf.at[f, c, to_z // 2], arecv.at[f, c, z],
                      s_send.at[f, c, to_z], a_recv.at[f, c, z], layer, to_z * RING + x)

    def copy_a(f, c, to_z, slot, to_layer):
        return remote(abuf.at[f, c, to_z // 2], arecv.at[f, c, slot],
                      a_send.at[f, c, to_z], a_recv.at[f, c, slot], to_layer, to_z * RING + x)

    def copy_b(f, c, to_x, slot):
        return remote(rows.at[f, c, slot], rows.at[f, c, slot],
                      b_send.at[f, c, to_x], b_recv.at[f, c, slot], layer, z * RING + to_x)

    def copy_c(f, to_x, slot):
        return remote(scales.at[f, slot], scales.at[f, slot],
                      c_send.at[f, to_x], c_recv.at[f, slot], layer, z * RING + to_x)

    def copy_h(f, to_place, slot, number):
        return remote(hid.at[slot, f], hid.at[slot, f], h_send.at[f, number], h_recv.at[f, slot],
                      layer, to_place)

    def copy_d(f, c, to_x, slot):
        return remote(part.at[f, c, to_x], drecv.at[f, c, slot],
                      d_send.at[f, c, to_x], d_recv.at[f, c, slot], layer, z * RING + to_x)

    def copy_e(f, c, to_z, slot):
        return remote(ebuf.at[f, c, to_z], erecv.at[f, c, slot],
                      e_send.at[f, c, to_z], e_recv.at[f, c, slot], layer, to_z * RING + x)

    def columns(c):
        return slice(c * part_width, (c + 1) * part_width)

    def copy_x(f, to_layer):
        return remote(xout.at[f], xin.at[f], x_send.at[f], x_recv.at[f], to_layer, place)

    def load_stream(f):
        return pltpu.make_async_copy(stream.at[f], xin.at[f], in_sem.at[f])

    def store_out(f):
        return pltpu.make_async_copy(xout.at[f], out.at[0, f], out_sem.at[f])

    weights = (
        pltpu.make_async_copy(wg.at[0], wg_v, w_sem.at[0]),
        pltpu.make_async_copy(wu.at[0], wu_v, w_sem.at[1]),
        pltpu.make_async_copy(wd.at[0], wd_v, w_sem.at[2]),
    )

    @pl.when(is_first)
    def _():
        for f in range(fronts):
            load_stream(f).start()

    for load in weights:
        load.start()

    barrier = pltpu.get_barrier_semaphore()

    def greet(to_layer, to_place):
        pl.semaphore_signal(barrier, inc=1, device_id=(to_layer, to_place), device_id_type=MESH)

    @pl.when(layer > 0)
    def _():
        for step in range(PLANES):
            greet(layer - 1, at_z(step) * RING + x)

    @pl.when(layer < sections - 1)
    def _():
        greet(layer + 1, place)

    for step in range(1, PLANES):
        greet(layer, at_z(step) * RING + x)
    for step in range(1, RING):
        greet(layer, z * RING + at_x(step))

    lanes = lax.broadcasted_iota(jnp.int32, (1, tokens), 1)
    row8 = lax.broadcasted_iota(jnp.int32, (flight * CAP, tokens), 0)
    row16 = lax.broadcasted_iota(jnp.int32, (2 * flight * CAP, tokens), 0)
    eye = (
        lax.broadcasted_iota(jnp.int32, (tokens, tokens), 0)
        == lax.broadcasted_iota(jnp.int32, (tokens, tokens), 1)
    ).astype(BF16)

    def own_tables(f):
        route, gate = routes[f], gates[f]
        pick = jnp.zeros((flight * CAP, tokens), F32)
        scaled = jnp.zeros((2 * flight * CAP, tokens), F32)
        for expert in range(flight):
            slots = first_and_second(route, expert, lanes)
            weight = jnp.sum(jnp.where(route == expert, gate, 0.0), axis=0, keepdims=True)
            for c in range(CAP):
                pick = jnp.where(row8 == expert * CAP + c, slots[c], pick)
                here = jnp.logical_and(row16 // (2 * CAP) == expert, row16 % CAP == c)
                scaled = jnp.where(here, slots[c] * weight, scaled)
        pick_own[f] = pick.astype(BF16)
        mix = scaled.T
        high = mix.astype(BF16)
        low = (mix - high.astype(F32)).astype(BF16)
        mix_full[f] = jnp.concatenate([eye, high, low], axis=1)

    def next_tables(f):
        route = routes_next[f]
        pick = jnp.zeros((flight * CAP, tokens), F32)
        for expert in range(flight):
            slots = first_and_second(route, expert, lanes)
            for c in range(CAP):
                pick = jnp.where(row8 == expert * CAP + c, slots[c], pick)
        mix_next[f] = jnp.dot(
            pick.astype(BF16), mix_full[f], preferred_element_type=F32
        ).astype(BF16)

    for f in range(fronts):
        own_tables(f)

    @pl.when(jnp.logical_and(is_first, is_last))
    def _():
        pl.semaphore_wait(barrier, 10)

    @pl.when(jnp.logical_and(is_first, jnp.logical_not(is_last)))
    def _():
        pl.semaphore_wait(barrier, 10 + PLANES)

    @pl.when(jnp.logical_and(jnp.logical_not(is_first), is_last))
    def _():
        pl.semaphore_wait(barrier, 10 + 1)

    @pl.when(jnp.logical_and(jnp.logical_not(is_first), jnp.logical_not(is_last)))
    def _():
        pl.semaphore_wait(barrier, 10 + 1 + PLANES)

    @pl.when(layer > 0)
    def _():
        copy_routes(layer - 1).start()

    def stage_s(f):
        load_stream(f).wait()
        for c in range(chunks):
            picked = jnp.dot(pick_own[f], xin[f, :, columns(c)], preferred_element_type=F32)
            sbuf[f, c] = picked.astype(BF16).reshape(flight, CAP, part_width)
            for step in range(1, PLANES):
                copy_s(f, c, at_z(step)).start()
            arecv[f, c, z] = sbuf[f, c, z // 2]

    def stage_a(f):
        squares = jnp.zeros((PLANES * CAP, 1), F32)
        for c in range(chunks):
            for step in range(1, PLANES):
                copy_a(f, c, z, at_z(step), layer).wait_recv()

            @pl.when(layer > 0)
            def _():
                copy_a(f, c, z, z, layer).wait_recv()

            wide = arecv[f, c].reshape(PLANES * CAP, part_width).astype(F32)
            rows[f, c, x] = (wide * gain[:, columns(c)]).astype(BF16)
            for step in (1, 3, 2):
                copy_b(f, c, at_x(step), x).start()
            squares = squares + jnp.sum(wide * wide, axis=-1, keepdims=True)
        scale = lax.rsqrt(squares * (1.0 / width) + EPSILON)
        scales[f, x] = jnp.broadcast_to(scale, scales.shape[2:])
        for step in (1, 3, 2):
            copy_c(f, at_x(step), x).start()

    def stage_b(f):
        count = RING * PLANES * CAP
        gate_act = jnp.zeros((count, wg_v.shape[1]), F32)
        up_act = jnp.zeros((count, wg_v.shape[1]), F32)
        for c in range(chunks):
            for step in range(1, RING):
                copy_b(f, c, x, at_x(step)).wait_recv()
            all_rows = rows[f, c].reshape(count, part_width)
            gate_act += jnp.dot(all_rows, wg_v[columns(c), :], preferred_element_type=F32)
            up_act += jnp.dot(all_rows, wu_v[columns(c), :], preferred_element_type=F32)
        for step in range(1, RING):
            copy_c(f, x, at_x(step)).wait_recv()
        scale = scales[f].reshape(count, scales.shape[-1])[:, :1]
        hidden = (jax.nn.silu(gate_act * scale) * (up_act * scale)).astype(BF16)
        for c in range(chunks):
            partial = jnp.dot(hidden, wd_v[:, columns(c)], preferred_element_type=F32)
            part[f, c] = partial.astype(BF16).reshape(RING, PLANES * CAP, part_width)
            for step in (1, 3, 2):
                copy_d(f, c, at_x(step), x).start()
        hid[member, f] = hidden
        copy_h(f, opposite, member, PLANES).start()
        for step in (1, 3, 2):
            copy_h(f, z * RING + at_x(step), half * RING + x, at_x(step)).start()

    def stage_h(f):
        for step in range(1, RING):
            slot = half * RING + at_x(step)
            copy_h(f, place, slot, PLANES).wait_recv()
            copy_h(f, opposite, slot, PLANES + step).start()

    def stage_d(f):
        for c in range(chunks):
            for step in range(1, RING):
                copy_d(f, c, x, at_x(step)).wait_recv()
            total = part[f, c, x].astype(F32)
            for step in range(1, RING):
                total = total + drecv[f, c, at_x(step)].astype(F32)
            ebuf[f, c] = total.astype(BF16).reshape(PLANES, CAP, part_width)
            for step in range(1, PLANES):
                copy_e(f, c, at_z(step), z).start()
            erecv[f, c, z] = ebuf[f, c, z]

    def stack(f, c):
        returned = erecv[f, c].reshape(PLANES * CAP, part_width)
        return jnp.concatenate([xin[f, :, columns(c)], returned, returned], axis=0)

    def stage_e(f):
        @pl.when(layer > 0)
        def _():
            copy_x(f, layer).wait_recv()

        for c in range(chunks):
            for step in range(1, PLANES):
                copy_e(f, c, z, at_z(step)).wait_recv()

            @pl.when(layer < sections - 1)
            def _():
                picked = jnp.dot(mix_next[f], stack(f, c), preferred_element_type=F32)
                abuf[f, c] = picked.astype(BF16).reshape(flight, CAP, part_width)
                for step in range(PLANES):
                    copy_a(f, c, at_z(step), z, layer + 1).start()

    def stage_u(f):
        for c in range(chunks):
            xout[f, :, columns(c)] = jnp.dot(
                mix_full[f], stack(f, c), preferred_element_type=F32
            ).astype(BF16)

        @pl.when(layer < sections - 1)
        def _():
            copy_x(f, layer + 1).start()

        store_out(f).start()

    @pl.when(is_first)
    def _():
        stage_s(0)

    @pl.when(layer < sections - 1)
    def _():
        copy_routes(layer).wait_recv()
        for f in range(fronts):
            next_tables(f)

    for load in weights:
        load.wait()

    stage_a(0)

    stage_b(0)

    def steady(f, carry):

        @pl.when(is_first)
        def _():
            stage_s(f + 1)

        stage_d(f)
        stage_a(f + 1)
        stage_e(f)
        stage_h(f)
        stage_b(f + 1)
        stage_u(f)
        return carry

    lax.fori_loop(0, fronts - 1, steady, 0)
    store_gram = pltpu.make_async_copy(gram, hess.at[0], hess_sem)

    def stage_gram():
        for f in range(fronts):
            for column in range(RING):
                copy_h(f, place, (1 - half) * RING + column, PLANES).wait_recv()
        mine = hid[member].reshape(-1, hid.shape[-1])
        units = hid.shape[-1]
        for slot in range(GROUP):
            theirs = hid[slot].reshape(-1, units)
            gram[:, slot * units:(slot + 1) * units] = lax.dot_general(
                mine, theirs, (((0,), (0,)), ((), ())), preferred_element_type=F32
            ) * (1.0 / (fronts * CAP))
        store_gram.start()

    last = fronts - 1
    stage_d(last)
    stage_h(last)
    stage_e(last)
    stage_u(last)
    stage_gram()

    @pl.when(layer > 0)
    def _():
        copy_routes(layer - 1).wait_send()

    def finish(f, carry):
        for step in range(1, RING):
            copy_c(f, at_x(step), x).wait_send()
        copy_h(f, opposite, member, PLANES).wait_send()
        for step in range(1, RING):
            copy_h(f, place, member, at_x(step)).wait_send()
            copy_h(f, opposite, member, PLANES + step).wait_send()
        for c in range(chunks):
            for step in range(1, RING):
                copy_b(f, c, at_x(step), x).wait_send()
                copy_d(f, c, at_x(step), x).wait_send()
            for step in range(1, PLANES):
                copy_e(f, c, at_z(step), z).wait_send()

        @pl.when(is_first)
        def _():
            for c in range(chunks):
                for step in range(1, PLANES):
                    copy_s(f, c, at_z(step)).wait_send()

        @pl.when(layer < sections - 1)
        def _():
            for c in range(chunks):
                for step in range(PLANES):
                    copy_a(f, c, at_z(step), z, layer + 1).wait_send()
            copy_x(f, layer + 1).wait_send()

        store_out(f).wait()
        return carry

    lax.fori_loop(0, fronts, finish, 0)
    store_gram.wait()


def shards(stream_in, gain, w_gate, w_up, w_down, routes, gates):
    fronts, tokens, width = stream_in.shape
    units = w_gate.shape[2]
    slots = PLANES * CAP
    flight = PLANES // 2
    part_width = width // CHUNKS
    dma = pltpu.SemaphoreType.DMA
    anywhere = pl.BlockSpec(memory_space=pl.ANY)
    vmem = pl.BlockSpec(memory_space=pltpu.VMEM)
    route_cols = jnp.swapaxes(routes[0], 1, 2)
    gate_cols = jnp.swapaxes(gates[0], 1, 2)
    return pl.pallas_call(
        kernel,
        out_shape=(
            jax.ShapeDtypeStruct((1, fronts, tokens, width), BF16),
            jax.ShapeDtypeStruct((1, units, GROUP * units), F32),
        ),
        in_specs=[anywhere, vmem, anywhere, anywhere, anywhere, vmem, vmem],
        out_specs=(anywhere, anywhere),
        scratch_shapes=[
            pltpu.VMEM((width, units), BF16),
            pltpu.VMEM((width, units), BF16),
            pltpu.VMEM((units, width), BF16),
            pltpu.VMEM(route_cols.shape, jnp.int32),
            pltpu.VMEM((fronts, flight * CAP, tokens), BF16),
            pltpu.VMEM((fronts, tokens, tokens + 2 * slots), BF16),
            pltpu.VMEM((fronts, flight * CAP, tokens + 2 * slots), BF16),
            pltpu.VMEM((fronts, tokens, width), BF16),
            pltpu.VMEM((fronts, tokens, width), BF16),
            pltpu.VMEM((fronts, CHUNKS, flight, CAP, part_width), BF16),
            pltpu.VMEM((fronts, CHUNKS, flight, CAP, part_width), BF16),
            pltpu.VMEM((fronts, CHUNKS, PLANES, CAP, part_width), BF16),
            pltpu.VMEM((fronts, RING, slots, 128), F32),
            pltpu.VMEM((fronts, CHUNKS, RING, slots, part_width), BF16),
            pltpu.VMEM((fronts, CHUNKS, RING, slots, part_width), BF16),
            pltpu.VMEM((fronts, CHUNKS, RING, slots, part_width), BF16),
            pltpu.VMEM((fronts, CHUNKS, PLANES, CAP, part_width), BF16),
            pltpu.VMEM((fronts, CHUNKS, PLANES, CAP, part_width), BF16),
            pltpu.VMEM((GROUP, fronts, RING * slots, units), BF16),
            pltpu.VMEM((units, GROUP * units), F32),
            dma((3,)), dma((fronts,)), dma((fronts,)), dma,
            dma, dma,
            dma((fronts, CHUNKS, PLANES)),
            dma((fronts, CHUNKS, PLANES)), dma((fronts, CHUNKS, PLANES)),
            dma((fronts, CHUNKS, RING)), dma((fronts, CHUNKS, RING)),
            dma((fronts, RING)), dma((fronts, RING)),
            dma((fronts, PLANES + RING)), dma((fronts, GROUP)),
            dma((fronts, CHUNKS, RING)), dma((fronts, CHUNKS, RING)),
            dma((fronts, CHUNKS, PLANES)), dma((fronts, CHUNKS, PLANES)),
            dma((fronts,)), dma((fronts,)),
        ],
        compiler_params=pltpu.CompilerParams(
            collective_id=0, has_side_effects=True, vmem_limit_bytes=60 * 1024 * 1024
        ),
    )(stream_in, gain, w_gate, w_up, w_down, route_cols, gate_cols)


def solution(mesh):
    return jax.shard_map(
        shards,
        mesh=mesh,
        in_specs=(
            P(None, "expert", None),
            P("layer", None),
            P("layer", None, "expert"),
            P("layer", None, "expert"),
            P("layer", "expert", None),
            P("layer", None, "expert", None),
            P("layer", None, "expert", None),
        ),
        out_specs=(P("layer", None, "expert", None), P("layer", "expert", None)),
        check_vma=False,
    )
```
